256 devices in a mesh: seq: 16 (over x_lo, y, core), head: 16 (over x_hi, z).
Axes of the slice: x: 4 (x_hi: 2, x_lo: 2; x = x_hi * 2 + x_lo), y: 4, z: 8, core: 2. Of those that a mesh axis runs over, the one named last changes fastest.
Arguments:
- query_heads: bfloat16 [16, 16384, 128], P('head', 'seq'), may hold values from -6 to 6
- key_heads: bfloat16 [2, 16384, 128], P(None, ('seq', 'head')), may hold values from -6 to 6
- value_heads: bfloat16 [2, 16384, 128], P(None, ('seq', 'head')), may hold values from -6 to 6
- doc_lengths: int32 [16], replicated, may hold values from 1 to 8192, 16384 in all
Outputs:
- attended: bfloat16 [16, 16384, 128], P('head', 'seq')
The draws below stay inside these ranges and needn't reach their ends.
Inputs may be any that keep to these rules, and one draw needn't show every extreme that they name: `doc_lengths`: the lengths sum to 16384; documents lie end to end in order.
All inputs are finite; a program needn't handle non-finite values.
Results may differ from the reference program's by a relative error of at most 0.0049.
Values may be sent and summed in bfloat16 or wider, within the bound.
A program may use at most 64 MiB of HBM per device.

```python
import math
import jax
import jax.numpy as jnp
import numpy as np
from jax import lax

HD = 128
QH = 16
KVH = 2
NDOCS = 16
SEQ = 16384
DOC_MOST = 8192


def draw_query_heads(key, part):
    noise_key, scale_key = jax.random.split(jax.random.fold_in(key, 3))
    base_draw = jax.random.normal(noise_key, (QH, SEQ, HD), jnp.float32)
    row_scale = jnp.exp(jax.random.uniform(scale_key, (QH, SEQ, 1), jnp.float32, math.log(0.3), math.log(3.0)))
    drawn = jnp.clip(base_draw * row_scale, -6.0, 6.0)
    return drawn.astype(jnp.bfloat16)


def draw_key_heads(key, part):
    noise_key = jax.random.fold_in(jax.random.fold_in(key, 5), 0)
    drawn = jnp.clip(jax.random.normal(noise_key, (KVH, SEQ, HD), jnp.float32), -6.0, 6.0)
    return drawn.astype(jnp.bfloat16)


def shard_levels(rng, dims, pieces, smallest, high):
    loudness, own = 1.0, jax.random.fold_in(rng, 6)
    for axis_at, parts in pieces:
        steps = jnp.exp(jax.random.uniform(jax.random.fold_in(own, axis_at), (parts,), jnp.float32, smallest / len(pieces), high / len(pieces)))
        loudness = loudness * jnp.repeat(steps, dims[axis_at] // parts).reshape([-1 if axis == axis_at else 1 for axis in range(len(dims))])
    return loudness


def length_profile(amount, total, reach, skew):
    weights = [(1 << 20) // math.isqrt(standing ** skew) + 1 for standing in range(2, amount + 1)]
    surplus, counts = total - reach - (amount - 1), [1] * (amount - 1)
    while surplus > 0:
        movable = [i for i in range(amount - 1) if counts[i] < reach]
        whole, left = sum([weights[i] for i in movable]), surplus
        for i in movable:
            more = min(reach - counts[i], max(1, left * weights[i] // whole), surplus)
            counts[i] = counts[i] + more
            surplus = surplus - more
    return np.array([reach] + counts)


def ragged(own_key, count, total, bound, slope):
    if count == 2:
        one = jax.random.randint(own_key, (), max(1, total - bound), min(bound, total - 1) + 1)
        return jnp.stack([one, total - one])
    sizes = jnp.asarray(length_profile(count, total, bound, slope), jnp.int32)
    twos = (count - 1) // 2
    giver, taker = sizes[1:1 + 2 * twos:2], sizes[2:2 + 2 * twos:2]
    slack = jnp.minimum(giver - 1, bound - taker)
    passed = jax.random.randint(jax.random.fold_in(own_key, 1), (twos,), 0, 1 << 20) % (slack + 1)
    sizes = sizes.at[1:1 + 2 * twos:2].set(giver - passed).at[2:2 + 2 * twos:2].set(taker + passed)
    return sizes[jax.random.permutation(jax.random.fold_in(own_key, 2), count)]


def scatter_about(key, extent, width, reach, cuts=(), held_as=jnp.bfloat16):
    values = width * jax.random.normal(key, extent, jnp.float32)
    if cuts:
        values = values * shard_levels(key, extent, cuts, -0.22, 0.18)
    return jnp.clip(values, -reach, reach).astype(held_as)


def setup_inputs(seed: int = 0) -> dict:
    key_of = jax.random.split(jax.random.key(seed), 5)
    return {
        "query_heads": draw_query_heads(jax.random.fold_in(key_of[4], 71), 0),
        "key_heads": draw_key_heads(jax.random.fold_in(key_of[4], 71), 0),
        "value_heads": scatter_about(key_of[2], (KVH, SEQ, HD), 1.0, 6.0, ((1, 256),)),
        "doc_lengths": ragged(key_of[3], NDOCS, SEQ, DOC_MOST, 2).astype(jnp.int32),
    }


NEG = -1e+30

def doc_first(doc_lengths, positions):
    doc_ends = jnp.cumsum(doc_lengths)
    starts = doc_ends - doc_lengths
    inside = starts[None, :] <= positions[:, None]
    return lax.optimization_barrier(jnp.max(jnp.where(inside, starts[None, :], 0), axis=1))

def reference(query_heads, key_heads, value_heads, doc_lengths):
    block_rows = math.gcd(512, SEQ)
    group_size = QH // KVH
    score_scale = 1.0 / math.sqrt(HD)
    key_pos = jnp.arange(SEQ, dtype=jnp.int32)

    def per_head(head_index):
        rows_all = lax.dynamic_index_in_dim(query_heads, head_index, 0, keepdims=False)
        key_all = lax.dynamic_index_in_dim(key_heads, head_index // group_size, 0, keepdims=False)
        value_all = lax.dynamic_index_in_dim(value_heads, head_index // group_size, 0, keepdims=False)

        def per_block(block_index):
            block_start = (block_index * block_rows).astype(jnp.int32)
            query_rows = lax.dynamic_slice_in_dim(rows_all, block_start, block_rows, 0)
            query_pos = block_start + jnp.arange(block_rows, dtype=jnp.int32)
            query_first = doc_first(doc_lengths, query_pos)
            scores = jnp.dot(query_rows, key_all.T, preferred_element_type=jnp.float32) * score_scale
            visible = (key_pos[None, :] <= query_pos[:, None]) & (key_pos[None, :] >= query_first[:, None])
            row_peak = lax.optimization_barrier(jnp.max(jnp.where(visible, scores, NEG), axis=1))
            weights = jnp.where(visible, jnp.exp(scores - row_peak[:, None]), 0.0)
            mixed_rows = jnp.dot(weights.astype(jnp.bfloat16), value_all, preferred_element_type=jnp.float32)
            return (mixed_rows / lax.optimization_barrier(jnp.sum(weights, axis=1))[:, None]).astype(jnp.bfloat16)
        blocks = lax.map(per_block, jnp.arange(SEQ // block_rows, dtype=jnp.int32))
        return blocks.reshape(SEQ, HD)
    return lax.map(per_head, jnp.arange(QH, dtype=jnp.int32))
```

```python
import functools
import math

import jax
import jax.numpy as jnp
from jax import lax
from jax.experimental import pallas as pl
from jax.experimental.pallas import tpu as pltpu
from jax.sharding import PartitionSpec as P

QH = 16
KVH = 2
HIDDEN = -1e30
LOG_SCALE = math.log2(math.e) / math.sqrt(128)
NT = (((1,), (1,)), ((), ()))
NN = (((1,), (0,)), ((), ()))


def attention_kernel(block, chunk, doc_ref, q_ref, kv_ref, o_ref, acc, peak, total, first):
    rows = q_ref.shape[0]
    start = lax.axis_index("seq") * rows
    peak[...] = jnp.full_like(peak, HIDDEN)
    total[...] = jnp.zeros_like(total)
    acc[...] = jnp.zeros_like(acc)
    pos = start + lax.broadcasted_iota(jnp.int32, (rows, 128), 0)
    doc_first = jnp.zeros((rows, 128), jnp.int32)
    low = jnp.int32(0)
    begin = jnp.int32(0)
    for d in range(doc_ref.shape[0]):
        doc_first = jnp.where(pos >= begin, begin, doc_first)
        low = jnp.where(start >= begin, begin, low)
        begin = begin + doc_ref[d]
    first[...] = doc_first

    def step(j, carry):
        base = pl.multiple_of(j * chunk, chunk)
        keys = kv_ref[0, pl.ds(base, chunk), :]
        values = kv_ref[1, pl.ds(base, chunk), :]
        lane = base + lax.broadcasted_iota(jnp.int32, (block, 128), 1)

        def score(i):
            return lax.dot_general(q_ref[pl.ds(i * block, block), :], keys, NT, preferred_element_type=jnp.float32)

        count = rows // block
        ahead = score(0)
        for i in range(count):
            s = ahead
            ahead = score(i + 1) if i + 1 < count else None
            r = pl.ds(i * block, block)
            f = first[r, :]
            line = start + i * block + lax.broadcasted_iota(jnp.int32, (block, 128), 0)
            cols = []
            for g in range(chunk // 128):
                key_pos = lane + g * 128
                cols.append(jnp.where((key_pos >= f) & (key_pos <= line), s[:, g * 128:(g + 1) * 128], HIDDEN))
            top = cols
            while len(top) > 1:
                top = [jnp.maximum(a, b) for a, b in zip(top[::2], top[1::2])]
            old = peak[r, :]
            new = jnp.maximum(old, jnp.max(top[0], axis=1, keepdims=True))
            shift = new * LOG_SCALE
            factor = jnp.exp2(old * LOG_SCALE - shift)
            peak[r, :] = new
            weights = [jnp.exp2(c * LOG_SCALE - shift) for c in cols]
            summed = weights
            while len(summed) > 1:
                summed = [a + b for a, b in zip(summed[::2], summed[1::2])]
            total[r, :] = total[r, :] * factor + summed[0]
            p = jnp.concatenate([w.astype(jnp.bfloat16) for w in weights], axis=1)
            acc[r, :] = acc[r, :] * factor + lax.dot_general(p, values, NN, preferred_element_type=jnp.float32)
        return carry

    lax.fori_loop(low // chunk, (start + rows) // chunk, step, 0)
    o_ref[...] = (acc[...] / jnp.sum(total[...], axis=1, keepdims=True)).astype(o_ref.dtype)


def local(query_heads, key_heads, value_heads, doc_lengths):
    heads_here, rows, width = query_heads.shape
    head_group = lax.axis_index("head") * heads_here // (QH // KVH)
    both = jnp.stack([key_heads, value_heads], axis=1)
    both = lax.all_gather(both, "head", axis=2, tiled=True)
    both = lax.dynamic_index_in_dim(both, head_group, 0, keepdims=False)
    both = lax.all_gather(both, "seq", axis=1, tiled=True)
    vmem = pl.BlockSpec(memory_space=pltpu.VMEM)
    out = pl.pallas_call(
        functools.partial(attention_kernel, 256, 1024),
        out_shape=jax.ShapeDtypeStruct((rows, width), jnp.bfloat16),
        in_specs=[pl.BlockSpec(memory_space=pltpu.SMEM), vmem, vmem],
        out_specs=vmem,
        scratch_shapes=[
            pltpu.VMEM((rows, width), jnp.float32),
            pltpu.VMEM((rows, 128), jnp.float32),
            pltpu.VMEM((rows, 128), jnp.float32),
            pltpu.VMEM((rows, 128), jnp.int32),
        ],
        compiler_params=pltpu.CompilerParams(vmem_limit_bytes=48 * 2**20),
        name="attention",
    )(doc_lengths, query_heads[0], both)
    return out[None]


def solution(mesh):
    placed = (
        P("head", "seq", None),
        P(None, ("seq", "head"), None),
        P(None, ("seq", "head"), None),
        P(),
    )
    return jax.shard_map(
        local, mesh=mesh, in_specs=placed, out_specs=P("head", "seq", None), check_vma=False
    )
```

```python
import math

import jax
import jax.numpy as jnp
from jax import lax
from jax.experimental import pallas as pl
from jax.experimental.pallas import tpu as pltpu
from jax.sharding import PartitionSpec as P

HIDDEN = -1e30
FAR = -(1 << 20)
LOG_SCALE = math.log2(math.e) / math.sqrt(128)
NT = (((1,), (1,)), ((), ()))
NN = (((1,), (0,)), ((), ()))
MESH = pl.DeviceIdType.MESH

SHARD = 1024
PIECE = 64
UNIT = 2 * PIECE
BLOCK = 256
OWN, OPPOSITE, BEHIND, AHEAD, ACROSS = range(5)
BACK = (0, 2, 1, 3, 4)
OFFSETS = (0, -1, 1, -2, 2, -3, 3, -4)
ROUNDS = ((0,), (1, 2), (3, 4), (5, 6), (7,))


def attention_kernel(
    doc_ref, q_ref, k_ref, v_ref, o_ref,
    even, odd, parcel, acc, peak, total, first,
    swap_sem, own_sem, opposite_sem, across_sem, behind_sem, ahead_sem, turn_sem, core_sem,
):
    seq, head = lax.axis_index("seq"), lax.axis_index("head")
    core, y, x = lax.rem(seq, 2), lax.rem(seq // 2, 4), seq // 8
    z, half = lax.rem(head, 8), head // 8

    def at(x_to, y_to, core_to=core):
        return ((x_to * 4 + y_to) * 2 + core_to, head)

    y_up, y_down = lax.rem(y + 1, 4), lax.rem(y + 3, 4)
    swap_to = (seq, (1 - half) * 8 + z)
    z_up_to = (seq, half * 8 + lax.rem(z + 1, 8))
    z_down_to = (seq, half * 8 + lax.rem(z + 7, 8))
    across_to = at(1 - x, y)
    up_to, down_to, turn_to = at(x, y_up), at(x, y_down), at(x, lax.rem(y + 2, 4))
    core_to = at(x, y, 1 - core)

    barrier = pltpu.get_barrier_semaphore()
    partners = (swap_to, z_up_to, z_down_to, across_to, up_to, down_to, turn_to, core_to)
    for partner in partners:
        pl.semaphore_signal(barrier, inc=1, device_id=partner, device_id_type=MESH)

    parcel[0] = k_ref[1 - half]
    parcel[1] = v_ref[1 - half]
    mine = pl.ds(pl.multiple_of(half * PIECE, PIECE), PIECE)
    even[z, OWN, 0, mine, :] = k_ref[half]
    even[z, OWN, 1, mine, :] = v_ref[half]
    pl.semaphore_wait(barrier, len(partners))

    slice_of = [lax.rem(z + off + 8, 8) for off in OFFSETS]

    def copy(src, dst, sems, index, to):
        return pltpu.make_async_remote_copy(
            src_ref=src, dst_ref=dst, send_sem=sems.at[0, index], recv_sem=sems.at[1, index],
            device_id=to, device_id_type=MESH,
        )

    swap_out = copy(parcel, even.at[z, OWN, :, mine, :], swap_sem, 0, swap_to)
    theirs = pl.ds(pl.multiple_of((1 - half) * PIECE, PIECE), PIECE)
    swap_in = copy(parcel, even.at[z, OWN, :, theirs, :], swap_sem, 0, swap_to)
    swap_out.start()

    def ring(slot, sems, u, unit, to):
        ref = even.at[slice_of[unit], slot]
        return copy(ref, ref, sems, u - 1, to)

    def ring_in(slot, sems, u):
        return ring(slot, sems, u, u, z_up_to)

    def ring_out(slot, sems, unit):
        out = []
        if OFFSETS[unit] <= 0 and OFFSETS[unit] > -4:
            u = OFFSETS.index(OFFSETS[unit] - 1)
            out.append(ring(slot, sems, u, unit, z_up_to))
        if OFFSETS[unit] >= 0 and OFFSETS[unit] < 3:
            u = OFFSETS.index(OFFSETS[unit] + 1)
            out.append(ring(slot, sems, u, unit, z_down_to))
        return out

    def across(u):
        return copy(even.at[slice_of[u], OWN], even.at[slice_of[u], ACROSS], across_sem, u, across_to)

    up_slot = jnp.where(y == 3, ACROSS, OWN)
    down_slot = jnp.where(y == 0, OWN, ACROSS)
    turn_slot = jnp.where(y < 2, OWN, ACROSS)

    def up(u):
        return copy(even.at[slice_of[u], up_slot], even.at[slice_of[u], BEHIND], behind_sem, u, up_to)

    def down(u):
        return copy(even.at[slice_of[u], down_slot], even.at[slice_of[u], AHEAD], ahead_sem, u, down_to)

    turn = copy(even.at[z, turn_slot], even.at[z, OPPOSITE], turn_sem, 0, turn_to)

    def to_core(u):
        return copy(even.at[slice_of[u], pl.ds(core, 4)], odd.at[slice_of[u]], core_sem, u, core_to)

    started = [swap_out]

    def send(copies):
        for one in copies:
            one.start()
            started.append(one)

    def own_arrives(step):
        for u in ROUNDS[step]:
            if u == 0:
                swap_in.wait_recv()
            else:
                ring_in(OWN, own_sem, u).wait_recv()
            send(ring_out(OWN, own_sem, u))
            send([across(u)])

    def across_arrives(step):
        for u in ROUNDS[step]:
            across(u).wait_recv()
            send([up(u), down(u)])
            if u == 0:
                send([turn])

    def opposite_arrives(step):
        for u in ROUNDS[step]:
            if u == 0:
                turn.wait_recv()
            else:
                ring_in(OPPOSITE, opposite_sem, u).wait_recv()
            send(ring_out(OPPOSITE, opposite_sem, u))

    def sides_arrive(step):
        for u in ROUNDS[step]:
            up(u).wait_recv()
            down(u).wait_recv()
            send([to_core(u)])

    def core_arrives(step):
        for u in ROUNDS[step]:
            to_core(u).wait_recv()

    chip = x * 4 + y
    start = seq * SHARD
    lane = lax.broadcasted_iota(jnp.int32, (1, 128), 1)
    place = jnp.where(lane < PIECE, lane, lane + (SHARD // 2 - PIECE))

    def base(slot, u, from_sibling):
        if from_sibling:
            back = jnp.where(core == 1, BACK[slot], BACK[slot + 1])
            owner = chip - back
            shard = owner * 2 + (1 - core)
        else:
            owner = chip - BACK[slot]
            shard = owner * 2 + core
        return jnp.where(owner >= 0, shard * SHARD + slice_of[u] * PIECE, FAR)

    def attend(keys, values, bases, causal, blocks):
        groups = len(bases)

        def score(i):
            return lax.dot_general(q_ref[0, pl.ds(i * BLOCK, BLOCK), :], keys, NT, preferred_element_type=jnp.float32)

        ahead = score(blocks[0])
        for n, i in enumerate(blocks):
            s = ahead
            ahead = score(blocks[n + 1]) if n + 1 < len(blocks) else None
            r = pl.ds(i * BLOCK, BLOCK)
            f = first[r, :]
            if causal:
                line = start + i * BLOCK + lax.broadcasted_iota(jnp.int32, (BLOCK, 128), 0) - place
            cols = []
            for g in range(groups):
                seen = f <= bases[g]
                if causal:
                    seen = seen & (line >= bases[g])
                cols.append(jnp.where(seen, s[:, g * UNIT:(g + 1) * UNIT], HIDDEN))
            top = tree(jnp.maximum, cols)
            old = peak[r, :]
            new = jnp.maximum(old, jnp.max(top, axis=1, keepdims=True))
            shift = new * LOG_SCALE
            factor = jnp.exp2(old * LOG_SCALE - shift)
            peak[r, :] = new
            weights = [jnp.exp2(c * LOG_SCALE - shift) for c in cols]
            total[r, :] = total[r, :] * factor + tree(jnp.add, weights)
            p = jnp.concatenate([w.astype(jnp.bfloat16) for w in weights], axis=1)
            acc[r, :] = acc[r, :] * factor + lax.dot_general(p, values, NN, preferred_element_type=jnp.float32)

    def attend_own(units):
        keys = jnp.concatenate([even[slice_of[u], OWN, 0] for u in units], axis=0)
        values = jnp.concatenate([even[slice_of[u], OWN, 1] for u in units], axis=0)
        attend(keys, values, [base(OWN, u, False) for u in units], True, (0, 1, 2, 3))

    def attend_others(step, blocks=(0, 1, 2, 3)):
        keys, values, bases = [], [], []
        for u in ROUNDS[step]:
            for ref, slots, sibling in ((even, range(1, 5), False), (odd, range(4), True)):
                for slot in slots:
                    keys.append(ref[slice_of[u], slot, 0])
                    values.append(ref[slice_of[u], slot, 1])
                    bases.append(base(slot, u, sibling))
        attend(jnp.concatenate(keys, axis=0), jnp.concatenate(values, axis=0), bases, False, blocks)

    peak[...] = jnp.full_like(peak, HIDDEN)
    total[...] = jnp.zeros_like(total)
    acc[...] = jnp.zeros_like(acc)
    pos = start + lax.broadcasted_iota(jnp.int32, (SHARD, 128), 0)
    doc_first = jnp.zeros((SHARD, 128), jnp.int32)
    begin = jnp.int32(0)
    for d in range(doc_ref.shape[0]):
        doc_first = jnp.where(pos >= begin, begin, doc_first)
        begin = begin + doc_ref[d]
    first[...] = doc_first - place

    own_arrives(0)
    across_arrives(0)
    own_arrives(1)
    attend_own((0, 1, 2))
    opposite_arrives(0)
    across_arrives(1)
    own_arrives(2)
    sides_arrive(0)
    opposite_arrives(1)
    across_arrives(2)
    own_arrives(3)
    core_arrives(0)
    attend_others(0)
    sides_arrive(1)
    opposite_arrives(2)
    across_arrives(3)
    own_arrives(4)
    attend_own((3, 4, 5, 6, 7))
    core_arrives(1)
    attend_others(1, (0, 1))
    sides_arrive(2)
    opposite_arrives(3)
    across_arrives(4)
    attend_others(1, (2, 3))
    sides_arrive(3)
    opposite_arrives(4)
    core_arrives(2)
    attend_others(2)
    sides_arrive(4)
    core_arrives(3)
    attend_others(3)
    core_arrives(4)
    attend_others(4)
    o_ref[0] = (acc[...] / jnp.sum(total[...], axis=1, keepdims=True)).astype(o_ref.dtype)
    for one in started:
        one.wait_send()


def tree(join, parts):
    while len(parts) > 1:
        rest = [parts[-1]] if len(parts) % 2 else []
        parts = [join(a, b) for a, b in zip(parts[::2], parts[1::2])] + rest
    return parts[0]


def local(query_heads, key_heads, value_heads, doc_lengths):
    _, rows, width = query_heads.shape
    vmem = pl.BlockSpec(memory_space=pltpu.VMEM)

    def sems(n):
        return pltpu.SemaphoreType.DMA((2, n))

    return pl.pallas_call(
        attention_kernel,
        out_shape=jax.ShapeDtypeStruct(query_heads.shape, jnp.bfloat16),
        in_specs=[pl.BlockSpec(memory_space=pltpu.SMEM), vmem, vmem, vmem],
        out_specs=vmem,
        scratch_shapes=[
            pltpu.VMEM((8, 5, 2, UNIT, width), jnp.bfloat16),
            pltpu.VMEM((8, 4, 2, UNIT, width), jnp.bfloat16),
            pltpu.VMEM((2, PIECE, width), jnp.bfloat16),
            pltpu.VMEM((rows, width), jnp.float32),
            pltpu.VMEM((rows, 128), jnp.float32),
            pltpu.VMEM((rows, 128), jnp.float32),
            pltpu.VMEM((rows, 128), jnp.int32),
            sems(1), sems(7), sems(7), sems(8), sems(8), sems(8), sems(1), sems(8),
        ],
        compiler_params=pltpu.CompilerParams(
            collective_id=0, has_side_effects=True, vmem_limit_bytes=48 * 2**20
        ),
        name="attention",
    )(doc_lengths, query_heads, key_heads, value_heads)


def solution(mesh):
    placed = (
        P("head", "seq", None),
        P(None, ("seq", "head"), None),
        P(None, ("seq", "head"), None),
        P(),
    )
    return jax.shard_map(
        local, mesh=mesh, in_specs=placed, out_specs=P("head", "seq", None), check_vma=False
    )
```

```python
import math

import jax
import jax.numpy as jnp
from jax import lax
from jax.experimental import pallas as pl
from jax.experimental.pallas import tpu as pltpu
from jax.sharding import PartitionSpec as P

HIDDEN = -1e30
FAR = -(1 << 20)
LOG_SCALE = math.log2(math.e) / math.sqrt(128)
NT = (((1,), (1,)), ((), ()))
NN = (((1,), (0,)), ((), ()))
MESH = pl.DeviceIdType.MESH

SHARD = 1024
PIECE = 64
UNIT = 2 * PIECE
BLOCK = 256
OWN, OPPOSITE, BEHIND, AHEAD, ACROSS = range(5)
BACK = (0, 2, 1, 3, 4)
OFFSETS = (0, -1, 1, -2, 2, -3, 3, -4)
ROUNDS = ((0,), (1, 2), (3, 4), (5, 6), (7,))


def attention_kernel(
    doc_ref, q_hbm, k_hbm, v_hbm, o_ref,
    even, odd, parcel, q_ref, acc, peak, total, first,
    load_sem, piece_sem, opposite_sem, relay_sem, start_sem, across_sem, behind_sem, ahead_sem, core_sem,
):
    seq, head = lax.axis_index("seq"), lax.axis_index("head")
    core, y, x = lax.rem(seq, 2), lax.rem(seq // 2, 4), seq // 8
    z, half = lax.rem(head, 8), head // 8
    chip = x * 4 + y
    halves = (half, 1 - half)

    def at(chip_to, core_to, half_to, z_to):
        return (lax.rem(chip_to, 8) * 2 + core_to, half_to * 8 + lax.rem(z_to, 8))

    def along(off):
        return at(chip, core, half, z + (off + 8))

    swap_to = at(chip, core, 1 - half, z)
    across_to = at(chip + 4, core, half, z)
    opposite_to = at(chip + 2, core, half, z)
    opposite_from = at(chip + 6, core, half, z)
    up_to = at(x * 4 + lax.rem(y + 1, 4), core, half, z)
    down_to = at(x * 4 + lax.rem(y + 3, 4), core, half, z)
    core_to = at(chip, 1 - core, half, z)

    mine = pl.ds(pl.multiple_of(half * PIECE, PIECE), PIECE)
    theirs = pl.ds(pl.multiple_of((1 - half) * PIECE, PIECE), PIECE)
    rows_of = (mine, theirs)
    loads = []
    for side in range(2):
        for n, ref in enumerate((k_hbm, v_hbm)):
            loads.append(pltpu.make_async_copy(ref.at[halves[side]], parcel.at[side, n], load_sem.at[side * 2 + n]))
    own_loads = [
        pltpu.make_async_copy(ref.at[half], even.at[z, OWN, n, mine, :], load_sem.at[4 + n])
        for n, ref in enumerate((k_hbm, v_hbm))
    ]
    q_load = pltpu.make_async_copy(q_hbm.at[0], q_ref, load_sem.at[6])
    for one in loads + own_loads + [q_load]:
        one.start()

    barrier = pltpu.get_barrier_semaphore()
    partners = (along(-1), along(1), along(-2), along(2), swap_to, across_to, up_to, down_to, opposite_from, core_to)
    for partner in partners:
        pl.semaphore_signal(barrier, inc=1, device_id=partner, device_id_type=MESH)

    start = seq * SHARD
    lane = lax.broadcasted_iota(jnp.int32, (1, 128), 1)
    place = jnp.where(lane < PIECE, lane, lane + (SHARD // 2 - PIECE))
    peak[...] = jnp.full_like(peak, HIDDEN)
    total[...] = jnp.zeros_like(total)
    acc[...] = jnp.zeros_like(acc)
    pos = start + lax.broadcasted_iota(jnp.int32, (SHARD, 128), 0)
    doc_first = jnp.zeros((SHARD, 128), jnp.int32)
    begin = jnp.int32(0)
    for d in range(doc_ref.shape[0]):
        doc_first = jnp.where(pos >= begin, begin, doc_first)
        begin = begin + doc_ref[d]
    first[...] = doc_first - place

    for one in loads:
        one.wait()
    pl.semaphore_wait(barrier, len(partners))

    slice_of = [lax.rem(z + off + 8, 8) for off in OFFSETS]
    started = []

    def copy(src, dst, sems, index, to):
        return pltpu.make_async_remote_copy(
            src_ref=src, dst_ref=dst, send_sem=sems.at[(0,) + index], recv_sem=sems.at[(1,) + index],
            device_id=to, device_id_type=MESH,
        )

    def send(copies):
        for one in copies:
            one.start()
            started.append(one)

    def swap(rows):
        return copy(parcel.at[1], even.at[z, OWN, :, rows, :], piece_sem, (1, 0), swap_to)

    def side_ref(u, side, slot=OWN):
        return even.at[slice_of[u], slot, :, rows_of[side], :]

    def side_source(side):
        return parcel.at[0] if side == 0 else side_ref(0, 1)

    def pieces_out(side):
        out = [
            copy(side_source(side), side_ref(0, side, slot), start_sem, (side, slot), to)
            for slot, to in ((ACROSS, across_to), (OPPOSITE, opposite_to))
        ]
        for u in (1, 2, 3, 4):
            out.append(copy(side_source(side), side_ref(0, side), piece_sem, (side, u), along(-OFFSETS[u])))
        return out

    def piece_in(u, side):
        return copy(side_source(side), side_ref(u, side), piece_sem, (side, u), along(OFFSETS[u]))

    def start_in(slot, side):
        return copy(side_source(side), side_ref(0, side, slot), start_sem, (side, slot), across_to)

    def spread(u, unit):
        ref = even.at[slice_of[unit], OPPOSITE]
        return copy(ref, ref, opposite_sem, (u - 1,), along(-OFFSETS[u]))

    def relay(slot, n, unit, off):
        ref = even.at[slice_of[unit], slot]
        if n >= 2:
            ref = ref.at[n - 2]
        return copy(ref, ref, relay_sem, (slot, n), along(off))

    def relays_out(slot, unit):
        if OFFSETS[unit] == -2:
            return [relay(slot, 0, unit, 1), relay(slot, 2, unit, 2)]
        if OFFSETS[unit] == 2:
            return [relay(slot, 1, unit, -1), relay(slot, 3, unit, -2)]
        return []

    def relays_in(slot, u):
        for n in {5: (0,), 6: (1,), 7: (2, 3)}[u]:
            relay(slot, n, u, 1).wait_recv()

    def across(u):
        return copy(even.at[slice_of[u], OWN], even.at[slice_of[u], ACROSS], across_sem, (u - 1,), across_to)

    up_slot = jnp.where(y == 3, ACROSS, OWN)
    down_slot = jnp.where(y == 0, OWN, ACROSS)

    def up(u):
        return copy(even.at[slice_of[u], up_slot], even.at[slice_of[u], BEHIND], behind_sem, (u,), up_to)

    def down(u):
        return copy(even.at[slice_of[u], down_slot], even.at[slice_of[u], AHEAD], ahead_sem, (u,), down_to)

    def to_core(u):
        return copy(even.at[slice_of[u], pl.ds(core, 4)], odd.at[slice_of[u]], core_sem, (u,), core_to)

    def own_arrives(step):
        for u in ROUNDS[step]:
            if u == 0:
                swap(theirs).wait_recv()
                send(pieces_out(1))
            elif u < 5:
                for side in range(2):
                    piece_in(u, side).wait_recv()
                send(relays_out(OWN, u))
            else:
                relays_in(OWN, u)
            if u:
                send([across(u)])

    def across_arrives(step):
        for u in ROUNDS[step]:
            if u:
                across(u).wait_recv()
            else:
                for side in range(2):
                    start_in(ACROSS, side).wait_recv()
            send([up(u), down(u)])

    def opposite_arrives(step):
        for u in ROUNDS[step]:
            if u == 0:
                for side in range(2):
                    start_in(OPPOSITE, side).wait_recv()
                send([spread(n, 0) for n in (1, 2, 3, 4)])
            elif u < 5:
                spread(u, u).wait_recv()
                send(relays_out(OPPOSITE, u))
            else:
                relays_in(OPPOSITE, u)

    def sides_arrive(step):
        for u in ROUNDS[step]:
            up(u).wait_recv()
            down(u).wait_recv()
            send([to_core(u)])

    def core_arrives(step):
        for u in ROUNDS[step]:
            to_core(u).wait_recv()

    send([swap(mine)])
    send(pieces_out(0))
    for one in own_loads + [q_load]:
        one.wait()

    def base(slot, u, from_sibling):
        if from_sibling:
            back = jnp.where(core == 1, BACK[slot], BACK[slot + 1])
            owner = chip - back
            shard = owner * 2 + (1 - core)
        else:
            owner = chip - BACK[slot]
            shard = owner * 2 + core
        return jnp.where(owner >= 0, shard * SHARD + slice_of[u] * PIECE, FAR)

    def attend(keys, values, bases, causal, blocks):
        groups = len(bases)

        def score(i):
            return lax.dot_general(q_ref[pl.ds(i * BLOCK, BLOCK), :], keys, NT, preferred_element_type=jnp.float32)

        ahead = score(blocks[0])
        for n, i in enumerate(blocks):
            s = ahead
            ahead = score(blocks[n + 1]) if n + 1 < len(blocks) else None
            r = pl.ds(i * BLOCK, BLOCK)
            f = first[r, :]
            if causal:
                line = start + i * BLOCK + lax.broadcasted_iota(jnp.int32, (BLOCK, 128), 0) - place
            cols = []
            for g in range(groups):
                seen = f <= bases[g]
                if causal:
                    seen = seen & (line >= bases[g])
                cols.append(jnp.where(seen, s[:, g * UNIT:(g + 1) * UNIT], HIDDEN))
            top = tree(jnp.maximum, cols)
            old = peak[r, :]
            new = jnp.maximum(old, jnp.max(top, axis=1, keepdims=True))
            shift = new * LOG_SCALE
            factor = jnp.exp2(old * LOG_SCALE - shift)
            peak[r, :] = new
            weights = [jnp.exp2(c * LOG_SCALE - shift) for c in cols]
            total[r, :] = total[r, :] * factor + tree(jnp.add, weights)
            p = jnp.concatenate([w.astype(jnp.bfloat16) for w in weights], axis=1)
            acc[r, :] = acc[r, :] * factor + lax.dot_general(p, values, NN, preferred_element_type=jnp.float32)

    def attend_own(units):
        keys = jnp.concatenate([even[slice_of[u], OWN, 0] for u in units], axis=0)
        values = jnp.concatenate([even[slice_of[u], OWN, 1] for u in units], axis=0)
        attend(keys, values, [base(OWN, u, False) for u in units], True, (0, 1, 2, 3))

    def attend_others(seen_even, seen_odd, blocks=(0, 1, 2, 3)):
        keys, values, bases = [], [], []
        for ref, slots, steps in ((even, range(1, 5), seen_even), (odd, range(4), seen_odd)):
            for u in [u for step in steps for u in ROUNDS[step]]:
                for slot in slots:
                    keys.append(ref[slice_of[u], slot, 0])
                    values.append(ref[slice_of[u], slot, 1])
                    bases.append(base(slot, u, ref is odd))
        attend(jnp.concatenate(keys, axis=0), jnp.concatenate(values, axis=0), bases, False, blocks)

    own_arrives(0)
    across_arrives(0)
    opposite_arrives(0)
    own_arrives(1)
    own_arrives(2)
    attend_own((0, 1, 2, 3, 4))
    sides_arrive(0)
    across_arrives(1)
    opposite_arrives(1)
    attend_others((0,), ())
    across_arrives(2)
    opposite_arrives(2)
    own_arrives(3)
    own_arrives(4)
    sides_arrive(1)
    core_arrives(0)
    attend_others((1,), (0,), (0, 1))
    sides_arrive(2)
    across_arrives(3)
    attend_others((1,), (0,), (2, 3))
    core_arrives(1)
    across_arrives(4)
    opposite_arrives(3)
    attend_others((2,), (1,), (0, 1))
    opposite_arrives(4)
    sides_arrive(3)
    attend_others((2,), (1,), (2, 3))
    sides_arrive(4)
    attend_own((5, 6, 7))
    core_arrives(2)
    attend_others((3, 4), (2,))
    core_arrives(3)
    core_arrives(4)
    attend_others((), (3, 4))
    o_ref[0] = (acc[...] / jnp.sum(total[...], axis=1, keepdims=True)).astype(o_ref.dtype)
    for one in started:
        one.wait_send()


def tree(join, parts):
    while len(parts) > 1:
        rest = [parts[-1]] if len(parts) % 2 else []
        parts = [join(a, b) for a, b in zip(parts[::2], parts[1::2])] + rest
    return parts[0]


def local(query_heads, key_heads, value_heads, doc_lengths):
    _, rows, width = query_heads.shape
    vmem = pl.BlockSpec(memory_space=pltpu.VMEM)

    hbm = pl.BlockSpec(memory_space=pltpu.HBM)

    def sems(*n):
        return pltpu.SemaphoreType.DMA((2,) + n)

    return pl.pallas_call(
        attention_kernel,
        out_shape=jax.ShapeDtypeStruct(query_heads.shape, jnp.bfloat16),
        in_specs=[pl.BlockSpec(memory_space=pltpu.SMEM), hbm, hbm, hbm],
        out_specs=vmem,
        scratch_shapes=[
            pltpu.VMEM((8, 5, 2, UNIT, width), jnp.bfloat16),
            pltpu.VMEM((8, 4, 2, UNIT, width), jnp.bfloat16),
            pltpu.VMEM((2, 2, PIECE, width), jnp.bfloat16),
            pltpu.VMEM((rows, width), jnp.bfloat16),
            pltpu.VMEM((rows, width), jnp.float32),
            pltpu.VMEM((rows, 128), jnp.float32),
            pltpu.VMEM((rows, 128), jnp.float32),
            pltpu.VMEM((rows, 128), jnp.int32),
            pltpu.SemaphoreType.DMA((7,)),
            sems(2, 5), sems(4), sems(2, 4), sems(2, 5), sems(7), sems(8), sems(8), sems(8),
        ],
        compiler_params=pltpu.CompilerParams(
            collective_id=0, has_side_effects=True, vmem_limit_bytes=48 * 2**20
        ),
        name="attention",
    )(doc_lengths, query_heads, key_heads, value_heads)


def solution(mesh):
    placed = (
        P("head", "seq", None),
        P(None, ("seq", "head"), None),
        P(None, ("seq", "head"), None),
        P(),
    )
    return jax.shard_map(
        local, mesh=mesh, in_specs=placed, out_specs=P("head", "seq", None), check_vma=False
    )
```

```python
import math

import jax
import jax.numpy as jnp
from jax import lax
from jax.experimental import pallas as pl
from jax.experimental.pallas import tpu as pltpu
from jax.sharding import PartitionSpec as P

HIDDEN = -1e30
FAR = -(1 << 20)
LOG_SCALE = math.log2(math.e) / math.sqrt(128)
NT = (((1,), (1,)), ((), ()))
NN = (((1,), (0,)), ((), ()))
MESH = pl.DeviceIdType.MESH

SHARD = 1024
PIECE = 64
UNIT = 2 * PIECE
BLOCK = 256
OWN, OPPOSITE, BEHIND, AHEAD, ACROSS = range(5)
BACK = (0, 2, 1, 3, 4)
OFFSETS = (0, -1, 1, -2, 2, -3, 3, -4)


def attention_kernel(
    doc_ref, q_hbm, k_hbm, v_hbm, o_ref,
    even, odd, parcel, q_ref, acc, peak, first,
    load_sem, piece_sem, opposite_sem, relay_sem, start_sem, across_sem, behind_sem, ahead_sem, core_sem,
):
    seq, head = lax.axis_index("seq"), lax.axis_index("head")
    core, y, x = lax.rem(seq, 2), lax.rem(seq // 2, 4), seq // 8
    z, half = lax.rem(head, 8), head // 8
    chip = x * 4 + y
    halves = (half, 1 - half)

    def at(chip_to, core_to, half_to, z_to):
        return (lax.rem(chip_to, 8) * 2 + core_to, half_to * 8 + lax.rem(z_to, 8))

    def along(off):
        return at(chip, core, half, z + (off + 8))

    swap_to = at(chip, core, 1 - half, z)
    across_to = at(chip + 4, core, half, z)
    opposite_to = at(chip + 2, core, half, z)
    opposite_from = at(chip + 6, core, half, z)
    up_to = at(x * 4 + lax.rem(y + 1, 4), core, half, z)
    down_to = at(x * 4 + lax.rem(y + 3, 4), core, half, z)
    core_to = at(chip, 1 - core, half, z)

    mine = pl.ds(pl.multiple_of(half * PIECE, PIECE), PIECE)
    theirs = pl.ds(pl.multiple_of((1 - half) * PIECE, PIECE), PIECE)
    rows_of = (mine, theirs)
    loads = []
    for side in range(2):
        for n, ref in enumerate((k_hbm, v_hbm)):
            loads.append(pltpu.make_async_copy(ref.at[halves[side]], parcel.at[side, n], load_sem.at[side * 2 + n]))
    own_loads = [
        pltpu.make_async_copy(ref.at[half], even.at[z, OWN, n, mine, :], load_sem.at[4 + n])
        for n, ref in enumerate((k_hbm, v_hbm))
    ]
    q_load = pltpu.make_async_copy(q_hbm.at[0], q_ref, load_sem.at[6])
    for one in loads + own_loads + [q_load]:
        one.start()

    barrier = pltpu.get_barrier_semaphore()
    partners = (along(-1), along(1), along(-2), along(2), swap_to, across_to, up_to, down_to, opposite_from, core_to)
    for partner in partners:
        pl.semaphore_signal(barrier, inc=1, device_id=partner, device_id_type=MESH)

    start = seq * SHARD
    lane = lax.broadcasted_iota(jnp.int32, (1, 128), 1)
    place = jnp.where(lane < PIECE, lane, lane + (SHARD // 2 - PIECE))
    peak[...] = jnp.full_like(peak, HIDDEN)
    acc[...] = jnp.zeros_like(acc)
    pos = start + lax.broadcasted_iota(jnp.int32, (SHARD, 128), 0)
    doc_first = jnp.zeros((SHARD, 128), jnp.int32)
    begin = jnp.int32(0)
    for d in range(doc_ref.shape[0]):
        doc_first = jnp.where(pos >= begin, begin, doc_first)
        begin = begin + doc_ref[d]
    first[...] = doc_first - place

    for one in loads:
        one.wait()
    pl.semaphore_wait(barrier, len(partners))

    slice_of = [lax.rem(z + off + 8, 8) for off in OFFSETS]
    started = []

    def copy(src, dst, sems, index, to):
        return pltpu.make_async_remote_copy(
            src_ref=src, dst_ref=dst, send_sem=sems.at[(0,) + index], recv_sem=sems.at[(1,) + index],
            device_id=to, device_id_type=MESH,
        )

    def send(copies):
        for one in copies:
            one.start()
            started.append(one)

    def swap(rows):
        return copy(parcel.at[1], even.at[z, OWN, :, rows, :], piece_sem, (1, 0), swap_to)

    def side_ref(u, side, slot=OWN):
        return even.at[slice_of[u], slot, :, rows_of[side], :]

    def side_source(side):
        return parcel.at[0] if side == 0 else side_ref(0, 1)

    def pieces_out(side):
        out = [
            copy(side_source(side), side_ref(0, side, slot), start_sem, (side, slot), to)
            for slot, to in ((ACROSS, across_to), (OPPOSITE, opposite_to))
        ]
        for u in (1, 2, 3, 4):
            out.append(copy(side_source(side), side_ref(0, side), piece_sem, (side, u), along(-OFFSETS[u])))
        return out

    def piece_in(u, side):
        return copy(side_source(side), side_ref(u, side), piece_sem, (side, u), along(OFFSETS[u]))

    def start_in(slot, side):
        return copy(side_source(side), side_ref(0, side, slot), start_sem, (side, slot), across_to)

    def spread(u, unit):
        ref = even.at[slice_of[unit], OPPOSITE]
        return copy(ref, ref, opposite_sem, (u - 1,), along(-OFFSETS[u]))

    def relay(slot, n, unit, off):
        ref = even.at[slice_of[unit], slot]
        if n >= 2:
            ref = ref.at[n - 2]
        return copy(ref, ref, relay_sem, (slot, n), along(off))

    def relays_out(slot, unit):
        if OFFSETS[unit] == -2:
            return [relay(slot, 0, unit, 1), relay(slot, 2, unit, 2)]
        if OFFSETS[unit] == 2:
            return [relay(slot, 1, unit, -1), relay(slot, 3, unit, -2)]
        return []

    def relays_in(slot, u):
        for n in {5: (0,), 6: (1,), 7: (2, 3)}[u]:
            relay(slot, n, u, 1).wait_recv()

    def across(u):
        return copy(even.at[slice_of[u], OWN], even.at[slice_of[u], ACROSS], across_sem, (u - 1,), across_to)

    up_slot = jnp.where(y == 3, ACROSS, OWN)
    down_slot = jnp.where(y == 0, OWN, ACROSS)

    def up(u):
        return copy(even.at[slice_of[u], up_slot], even.at[slice_of[u], BEHIND], behind_sem, (u,), up_to)

    def down(u):
        return copy(even.at[slice_of[u], down_slot], even.at[slice_of[u], AHEAD], ahead_sem, (u,), down_to)

    def to_core(u):
        return copy(even.at[slice_of[u], pl.ds(core, 4)], odd.at[slice_of[u]], core_sem, (u,), core_to)

    def own_arrives(*units):
        for u in units:
            if u == 0:
                swap(theirs).wait_recv()
                send(pieces_out(1))
            elif u < 5:
                for side in range(2):
                    piece_in(u, side).wait_recv()
                send(relays_out(OWN, u))
            else:
                relays_in(OWN, u)
            if u:
                send([across(u)])

    def across_arrives(*units):
        for u in units:
            if u:
                across(u).wait_recv()
            else:
                for side in range(2):
                    start_in(ACROSS, side).wait_recv()
            send([up(u), down(u)])

    def opposite_arrives(*units):
        for u in units:
            if u == 0:
                for side in range(2):
                    start_in(OPPOSITE, side).wait_recv()
                send([spread(n, 0) for n in (1, 2, 3, 4)])
            elif u < 5:
                spread(u, u).wait_recv()
                send(relays_out(OPPOSITE, u))
            else:
                relays_in(OPPOSITE, u)

    def sides_arrive(*units):
        for u in units:
            up(u).wait_recv()
            down(u).wait_recv()
            send([to_core(u)])

    def core_arrives(*units):
        for u in units:
            to_core(u).wait_recv()

    send([swap(mine)])
    send(pieces_out(0))
    for one in own_loads + [q_load]:
        one.wait()

    def base(slot, u, from_sibling):
        if from_sibling:
            back = jnp.where(core == 1, BACK[slot], BACK[slot + 1])
            owner = chip - back
            shard = owner * 2 + (1 - core)
        else:
            owner = chip - BACK[slot]
            shard = owner * 2 + core
        return jnp.where(owner >= 0, shard * SHARD + slice_of[u] * PIECE, FAR)

    def attend(keys, values, bases, causal, blocks):
        groups = len(bases)
        values = jnp.concatenate([values, jnp.ones_like(values)], axis=1)

        def score(i):
            return lax.dot_general(q_ref[pl.ds(i * BLOCK, BLOCK), :], keys, NT, preferred_element_type=jnp.float32)

        ahead = score(blocks[0])
        for n, i in enumerate(blocks):
            s = ahead
            ahead = score(blocks[n + 1]) if n + 1 < len(blocks) else None
            r = pl.ds(i * BLOCK, BLOCK)
            f = first[r, :]
            if causal:
                line = start + i * BLOCK + lax.broadcasted_iota(jnp.int32, (BLOCK, 128), 0) - place
            cols = []
            for g in range(groups):
                seen = f <= bases[g]
                if causal:
                    seen = seen & (line >= bases[g])
                cols.append(jnp.where(seen, s[:, g * UNIT:(g + 1) * UNIT], HIDDEN))
            top = tree(jnp.maximum, cols)
            old = peak[r, :]
            new = jnp.maximum(old, jnp.max(top, axis=1, keepdims=True))
            shift = new * LOG_SCALE
            factor = jnp.exp2(old * LOG_SCALE - shift)
            peak[r, :] = new
            weights = [jnp.exp2(c * LOG_SCALE - shift) for c in cols]
            p = jnp.concatenate([w.astype(jnp.bfloat16) for w in weights], axis=1)
            product = lax.dot_general(p, values, NN, preferred_element_type=jnp.float32)
            for part in (pl.ds(0, 128), pl.ds(128, 128)):
                acc[r, part] = acc[r, part] * factor + product[:, part.start:part.start + 128]

    def attend_own(units):
        keys, values = [[even[slice_of[u], OWN, n, pl.ds(0, PIECE)] for u in units] for n in range(2)]
        bases = [
            jnp.where(lane < PIECE, base(OWN, a, False), base(OWN, b, False) - SHARD // 2)
            for a, b in zip(units[::2], units[1::2])
        ]
        attend(jnp.concatenate(keys, axis=0), jnp.concatenate(values, axis=0), bases, True, (0, 1))
        keys, values = [[even[slice_of[u], OWN, n] for u in units] for n in range(2)]
        bases = [base(OWN, u, False) for u in units]
        attend(jnp.concatenate(keys, axis=0), jnp.concatenate(values, axis=0), bases, True, (2, 3))

    def attend_others(seen_even, seen_odd, blocks=(0, 1, 2, 3)):
        keys, values, bases = [], [], []
        for ref, slots, units in ((even, range(1, 5), seen_even), (odd, range(4), seen_odd)):
            for u in units:
                for slot in slots:
                    keys.append(ref[slice_of[u], slot, 0])
                    values.append(ref[slice_of[u], slot, 1])
                    bases.append(base(slot, u, ref is odd))
        attend(jnp.concatenate(keys, axis=0), jnp.concatenate(values, axis=0), bases, False, blocks)

    own_arrives(0)
    own_arrives(1)
    own_arrives(2)
    own_arrives(3)
    own_arrives(4)
    across_arrives(0)
    opposite_arrives(0)
    attend_own((0, 1, 2, 3))
    across_arrives(1)
    across_arrives(2)
    own_arrives(5)
    own_arrives(6)
    own_arrives(7)
    sides_arrive(0)
    attend_others((0,), ())
    across_arrives(3)
    across_arrives(4)
    opposite_arrives(1, 2)
    opposite_arrives(3, 4)
    attend_own((4, 5, 6, 7))
    sides_arrive(1)
    sides_arrive(2)
    core_arrives(0)
    attend_others((1, 2), (0,), (0, 1))
    across_arrives(5)
    across_arrives(6)
    across_arrives(7)
    attend_others((1, 2), (0,), (2, 3))
    sides_arrive(3)
    sides_arrive(4)
    opposite_arrives(5, 6, 7)
    core_arrives(1, 2)
    attend_others((3, 4), (1, 2), (0, 1))
    sides_arrive(5)
    sides_arrive(6)
    sides_arrive(7)
    attend_others((3, 4), (1, 2), (2, 3))
    core_arrives(3, 4)
    attend_others((5, 6, 7), (3, 4))
    core_arrives(5, 6, 7)
    attend_others((), (5, 6, 7))
    o_ref[0] = (acc[:, :128] / acc[:, 128:]).astype(o_ref.dtype)
    for one in started:
        one.wait_send()


def tree(join, parts):
    while len(parts) > 1:
        rest = [parts[-1]] if len(parts) % 2 else []
        parts = [join(a, b) for a, b in zip(parts[::2], parts[1::2])] + rest
    return parts[0]


def local(query_heads, key_heads, value_heads, doc_lengths):
    _, rows, width = query_heads.shape
    vmem = pl.BlockSpec(memory_space=pltpu.VMEM)

    hbm = pl.BlockSpec(memory_space=pltpu.HBM)

    def sems(*n):
        return pltpu.SemaphoreType.DMA((2,) + n)

    return pl.pallas_call(
        attention_kernel,
        out_shape=jax.ShapeDtypeStruct(query_heads.shape, jnp.bfloat16),
        in_specs=[pl.BlockSpec(memory_space=pltpu.SMEM), hbm, hbm, hbm],
        out_specs=vmem,
        scratch_shapes=[
            pltpu.VMEM((8, 5, 2, UNIT, width), jnp.bfloat16),
            pltpu.VMEM((8, 4, 2, UNIT, width), jnp.bfloat16),
            pltpu.VMEM((2, 2, PIECE, width), jnp.bfloat16),
            pltpu.VMEM((rows, width), jnp.bfloat16),
            pltpu.VMEM((rows, 2 * width), jnp.float32),
            pltpu.VMEM((rows, 128), jnp.float32),
            pltpu.VMEM((rows, 128), jnp.int32),
            pltpu.SemaphoreType.DMA((7,)),
            sems(2, 5), sems(4), sems(2, 4), sems(2, 5), sems(7), sems(8), sems(8), sems(8),
        ],
        compiler_params=pltpu.CompilerParams(
            collective_id=0, has_side_effects=True, vmem_limit_bytes=48 * 2**20
        ),
        name="attention",
    )(doc_lengths, query_heads, key_heads, value_heads)


def solution(mesh):
    placed = (
        P("head", "seq", None),
        P(None, ("seq", "head"), None),
        P(None, ("seq", "head"), None),
        P(),
    )
    return jax.shard_map(
        local, mesh=mesh, in_specs=placed, out_specs=P("head", "seq", None), check_vma=False
    )
```

```python
import math

import jax
import jax.numpy as jnp
from jax import lax
from jax.experimental import pallas as pl
from jax.experimental.pallas import tpu as pltpu
from jax.sharding import PartitionSpec as P

HIDDEN = -1e30
FAR = -(1 << 20)
LOG_SCALE = math.log2(math.e) / math.sqrt(128)
NT = (((1,), (1,)), ((), ()))
NN = (((1,), (0,)), ((), ()))
MESH = pl.DeviceIdType.MESH

SHARD = 1024
PIECE = 64
UNIT = 2 * PIECE
BLOCK = 256
OWN, OPPOSITE, BEHIND, AHEAD, ACROSS = range(5)
BACK = (0, 2, 1, 3, 4)
OFFSETS = (0, -1, 1, -2, 2, -3, 3, -4)


def attention_kernel(
    doc_ref, q_hbm, k_hbm, v_hbm, o_ref,
    even, odd, parcel, q_ref, acc, peak, first,
    load_sem, piece_sem, opposite_sem, relay_sem, start_sem, across_sem, behind_sem, ahead_sem, core_sem,
):
    seq, head = lax.axis_index("seq"), lax.axis_index("head")
    core, y, x = lax.rem(seq, 2), lax.rem(seq // 2, 4), seq // 8
    z, half = lax.rem(head, 8), head // 8
    chip = x * 4 + y
    halves = (half, 1 - half)

    def at(chip_to, core_to, half_to, z_to):
        return (lax.rem(chip_to, 8) * 2 + core_to, half_to * 8 + lax.rem(z_to, 8))

    def along(off):
        return at(chip, core, half, z + (off + 8))

    swap_to = at(chip, core, 1 - half, z)
    across_to = at(chip + 4, core, half, z)
    opposite_to = at(chip + 2, core, half, z)
    opposite_from = at(chip + 6, core, half, z)
    up_to = at(x * 4 + lax.rem(y + 1, 4), core, half, z)
    down_to = at(x * 4 + lax.rem(y + 3, 4), core, half, z)
    core_to = at(chip, 1 - core, half, z)

    mine = pl.ds(pl.multiple_of(half * PIECE, PIECE), PIECE)
    theirs = pl.ds(pl.multiple_of((1 - half) * PIECE, PIECE), PIECE)
    rows_of = (mine, theirs)
    loads = []
    for side in range(2):
        for n, ref in enumerate((k_hbm, v_hbm)):
            loads.append(pltpu.make_async_copy(ref.at[halves[side]], parcel.at[side, n], load_sem.at[side * 2 + n]))
    own_loads = [
        pltpu.make_async_copy(ref.at[half], even.at[z, OWN, n, mine, :], load_sem.at[4 + n])
        for n, ref in enumerate((k_hbm, v_hbm))
    ]
    q_load = pltpu.make_async_copy(q_hbm.at[0], q_ref, load_sem.at[6])
    for one in loads + own_loads + [q_load]:
        one.start()

    barrier = pltpu.get_barrier_semaphore()
    partners = (along(-1), along(1), along(-2), along(2), swap_to, across_to, up_to, down_to, opposite_from, core_to)
    for partner in partners:
        pl.semaphore_signal(barrier, inc=1, device_id=partner, device_id_type=MESH)

    start = seq * SHARD
    lane = lax.broadcasted_iota(jnp.int32, (1, 128), 1)
    place = jnp.where(lane < PIECE, lane, lane + (SHARD // 2 - PIECE))
    peak[...] = jnp.full_like(peak, HIDDEN)
    acc[...] = jnp.zeros_like(acc)
    pos = start + lax.broadcasted_iota(jnp.int32, (SHARD, 128), 0)
    doc_first = jnp.zeros((SHARD, 128), jnp.int32)
    begin = jnp.int32(0)
    for d in range(doc_ref.shape[0]):
        doc_first = jnp.where(pos >= begin, begin, doc_first)
        begin = begin + doc_ref[d]
    first[...] = doc_first - place

    for one in loads:
        one.wait()
    pl.semaphore_wait(barrier, len(partners))

    slice_of = [lax.rem(z + off + 8, 8) for off in OFFSETS]
    started = []

    def copy(src, dst, sems, index, to):
        return pltpu.make_async_remote_copy(
            src_ref=src, dst_ref=dst, send_sem=sems.at[(0,) + index], recv_sem=sems.at[(1,) + index],
            device_id=to, device_id_type=MESH,
        )

    def send(copies):
        for one in copies:
            one.start()
            started.append(one)

    def swap(rows):
        return copy(parcel.at[1], even.at[z, OWN, :, rows, :], piece_sem, (1, 0), swap_to)

    def side_ref(u, side, slot=OWN):
        return even.at[slice_of[u], slot, :, rows_of[side], :]

    def side_source(side):
        return parcel.at[0] if side == 0 else side_ref(0, 1)

    def pieces_out(side):
        out = [
            copy(side_source(side), side_ref(0, side, slot), start_sem, (side, slot), to)
            for slot, to in ((ACROSS, across_to), (OPPOSITE, opposite_to))
        ]
        for u in (1, 2, 3, 4):
            out.append(copy(side_source(side), side_ref(0, side), piece_sem, (side, u), along(-OFFSETS[u])))
        return out

    def piece_in(u, side):
        return copy(side_source(side), side_ref(u, side), piece_sem, (side, u), along(OFFSETS[u]))

    def start_in(slot, side):
        return copy(side_source(side), side_ref(0, side, slot), start_sem, (side, slot), across_to)

    def spread(u, unit):
        ref = even.at[slice_of[unit], OPPOSITE]
        return copy(ref, ref, opposite_sem, (u - 1,), along(-OFFSETS[u]))

    def relay(slot, n, unit, off):
        ref = even.at[slice_of[unit], slot]
        if n >= 2:
            ref = ref.at[n - 2]
        return copy(ref, ref, relay_sem, (slot, n), along(off))

    def relays_out(slot, unit):
        if OFFSETS[unit] == -2:
            return [relay(slot, 0, unit, 1), relay(slot, 2, unit, 2)]
        if OFFSETS[unit] == 2:
            return [relay(slot, 1, unit, -1), relay(slot, 3, unit, -2)]
        return []

    def relays_in(slot, u):
        for n in {5: (0,), 6: (1,), 7: (2, 3)}[u]:
            relay(slot, n, u, 1).wait_recv()

    def across(u):
        return copy(even.at[slice_of[u], OWN], even.at[slice_of[u], ACROSS], across_sem, (u - 1,), across_to)

    up_slot = jnp.where(y == 3, ACROSS, OWN)
    down_slot = jnp.where(y == 0, OWN, ACROSS)

    def up(u):
        return copy(even.at[slice_of[u], up_slot], even.at[slice_of[u], BEHIND], behind_sem, (u,), up_to)

    def down(u):
        return copy(even.at[slice_of[u], down_slot], even.at[slice_of[u], AHEAD], ahead_sem, (u,), down_to)

    def to_core(u):
        return copy(even.at[slice_of[u], pl.ds(core, 4)], odd.at[slice_of[u]], core_sem, (u,), core_to)

    def own_arrives(*units):
        for u in units:
            if u == 0:
                swap(theirs).wait_recv()
                send(pieces_out(1))
            elif u < 5:
                for side in range(2):
                    piece_in(u, side).wait_recv()
                send(relays_out(OWN, u))
            else:
                relays_in(OWN, u)
            if u:
                send([across(u)])

    def across_arrives(*units):
        for u in units:
            if u:
                across(u).wait_recv()
            else:
                for side in range(2):
                    start_in(ACROSS, side).wait_recv()
            send([up(u), down(u)])

    def opposite_arrives(*units):
        for u in units:
            if u == 0:
                for side in range(2):
                    start_in(OPPOSITE, side).wait_recv()
                send([spread(n, 0) for n in (1, 2, 3, 4)])
            elif u < 5:
                spread(u, u).wait_recv()
                send(relays_out(OPPOSITE, u))
            else:
                relays_in(OPPOSITE, u)

    def sides_arrive(*units):
        for u in units:
            up(u).wait_recv()
            down(u).wait_recv()
            send([to_core(u)])

    def core_arrives(*units):
        for u in units:
            to_core(u).wait_recv()

    send([swap(mine)])
    send(pieces_out(0))
    for one in own_loads + [q_load]:
        one.wait()

    def base(slot, u, from_sibling):
        if from_sibling:
            back = jnp.where(core == 1, BACK[slot], BACK[slot + 1])
            owner = chip - back
            shard = owner * 2 + (1 - core)
        else:
            owner = chip - BACK[slot]
            shard = owner * 2 + core
        return jnp.where(owner >= 0, shard * SHARD + slice_of[u] * PIECE, FAR)

    def attend(keys, values, bases, causal, blocks, block=BLOCK):
        groups = len(bases)
        values = jnp.concatenate([values, jnp.ones_like(values)], axis=1)

        def score(i):
            return lax.dot_general(q_ref[pl.ds(i * block, block), :], keys, NT, preferred_element_type=jnp.float32)

        ahead = score(blocks[0])
        for n, i in enumerate(blocks):
            s = ahead
            ahead = score(blocks[n + 1]) if n + 1 < len(blocks) else None
            r = pl.ds(i * block, block)
            f = first[r, :]
            if causal:
                line = start + i * block + lax.broadcasted_iota(jnp.int32, (block, 128), 0) - place
            cols = []
            for g in range(groups):
                seen = f <= bases[g]
                if causal:
                    seen = seen & (line >= bases[g])
                cols.append(jnp.where(seen, s[:, g * UNIT:(g + 1) * UNIT], HIDDEN))
            top = tree(jnp.maximum, cols)
            old = peak[r, :]
            new = jnp.maximum(old, jnp.max(top, axis=1, keepdims=True))
            shift = new * LOG_SCALE
            factor = jnp.exp2(old * LOG_SCALE - shift)
            peak[r, :] = new
            weights = [jnp.exp2(c * LOG_SCALE - shift) for c in cols]
            p = jnp.concatenate([w.astype(jnp.bfloat16) for w in weights], axis=1)
            product = lax.dot_general(p, values, NN, preferred_element_type=jnp.float32)
            for part in (pl.ds(0, 128), pl.ds(128, 128)):
                acc[r, part] = acc[r, part] * factor + product[:, part.start:part.start + 128]

    def attend_own(units):
        keys, values = [[even[slice_of[u], OWN, n, pl.ds(0, PIECE)] for u in units] for n in range(2)]
        bases = [
            jnp.where(lane < PIECE, base(OWN, a, False), base(OWN, b, False) - SHARD // 2)
            for a, b in zip(units[::2], units[1::2])
        ]
        attend(jnp.concatenate(keys, axis=0), jnp.concatenate(values, axis=0), bases, True, (0, 1))
        keys, values = [[even[slice_of[u], OWN, n] for u in units] for n in range(2)]
        bases = [base(OWN, u, False) for u in units]
        attend(jnp.concatenate(keys, axis=0), jnp.concatenate(values, axis=0), bases, True, (2, 3))

    def attend_others(seen_even, seen_odd, blocks=(0, 1, 2, 3), block=BLOCK):
        keys, values, bases = [], [], []
        for ref, slots, units in ((even, range(1, 5), seen_even), (odd, range(4), seen_odd)):
            for u in units:
                for slot in slots:
                    keys.append(ref[slice_of[u], slot, 0])
                    values.append(ref[slice_of[u], slot, 1])
                    bases.append(base(slot, u, ref is odd))
        attend(jnp.concatenate(keys, axis=0), jnp.concatenate(values, axis=0), bases, False, blocks, block)

    own_arrives(0)
    own_arrives(1)
    own_arrives(2)
    own_arrives(3)
    own_arrives(4)
    across_arrives(0)
    opposite_arrives(0)
    attend_own((0, 1, 2, 3))
    across_arrives(1)
    across_arrives(2)
    own_arrives(5)
    own_arrives(6)
    own_arrives(7)
    sides_arrive(0)
    attend_others((0,), ())
    across_arrives(3)
    across_arrives(4)
    opposite_arrives(1, 2)
    opposite_arrives(3, 4)
    attend_own((4, 5, 6, 7))
    sides_arrive(1)
    sides_arrive(2)
    core_arrives(0)
    attend_others((1, 2), (0,), (0, 1))
    across_arrives(5)
    across_arrives(6)
    across_arrives(7)
    attend_others((1, 2), (0,), (2, 3))
    sides_arrive(3)
    sides_arrive(4)
    opposite_arrives(5, 6, 7)
    core_arrives(1, 2)
    attend_others((3, 4), (1, 2), (0, 1))
    sides_arrive(5)
    sides_arrive(6)
    sides_arrive(7)
    attend_others((3, 4), (1, 2), (2, 3))
    core_arrives(3, 4)
    attend_others((5, 6, 7), (3, 4), (0, 1), 2 * BLOCK)
    core_arrives(5, 6, 7)
    attend_others((), (5, 6, 7), (0, 1), 2 * BLOCK)
    o_ref[0] = (acc[:, :128] / acc[:, 128:]).astype(o_ref.dtype)
    for one in started:
        one.wait_send()


def tree(join, parts):
    while len(parts) > 1:
        rest = [parts[-1]] if len(parts) % 2 else []
        parts = [join(a, b) for a, b in zip(parts[::2], parts[1::2])] + rest
    return parts[0]


def local(query_heads, key_heads, value_heads, doc_lengths):
    _, rows, width = query_heads.shape
    vmem = pl.BlockSpec(memory_space=pltpu.VMEM)

    hbm = pl.BlockSpec(memory_space=pltpu.HBM)

    def sems(*n):
        return pltpu.SemaphoreType.DMA((2,) + n)

    return pl.pallas_call(
        attention_kernel,
        out_shape=jax.ShapeDtypeStruct(query_heads.shape, jnp.bfloat16),
        in_specs=[pl.BlockSpec(memory_space=pltpu.SMEM), hbm, hbm, hbm],
        out_specs=vmem,
        scratch_shapes=[
            pltpu.VMEM((8, 5, 2, UNIT, width), jnp.bfloat16),
            pltpu.VMEM((8, 4, 2, UNIT, width), jnp.bfloat16),
            pltpu.VMEM((2, 2, PIECE, width), jnp.bfloat16),
            pltpu.VMEM((rows, width), jnp.bfloat16),
            pltpu.VMEM((rows, 2 * width), jnp.float32),
            pltpu.VMEM((rows, 128), jnp.float32),
            pltpu.VMEM((rows, 128), jnp.int32),
            pltpu.SemaphoreType.DMA((7,)),
            sems(2, 5), sems(4), sems(2, 4), sems(2, 5), sems(7), sems(8), sems(8), sems(8),
        ],
        compiler_params=pltpu.CompilerParams(
            collective_id=0, has_side_effects=True, vmem_limit_bytes=65000 * 2**10
        ),
        name="attention",
    )(doc_lengths, query_heads, key_heads, value_heads)


def solution(mesh):
    placed = (
        P("head", "seq", None),
        P(None, ("seq", "head"), None),
        P(None, ("seq", "head"), None),
        P(),
    )
    return jax.shard_map(
        local, mesh=mesh, in_specs=placed, out_specs=P("head", "seq", None), check_vma=False
    )
```

```python
import math

import jax
import jax.numpy as jnp
from jax import lax
from jax.experimental import pallas as pl
from jax.experimental.pallas import tpu as pltpu
from jax.sharding import PartitionSpec as P

HIDDEN = -1e30
FAR = -(1 << 20)
LOG_SCALE = math.log2(math.e) / math.sqrt(128)
NT = (((1,), (1,)), ((), ()))
NN = (((1,), (0,)), ((), ()))
MESH = pl.DeviceIdType.MESH

SHARD = 1024
PIECE = 64
UNIT = 2 * PIECE
BLOCK = 256
OWN, OPPOSITE, BEHIND, AHEAD, ACROSS = range(5)
BACK = (0, 2, 1, 3, 4)
OFFSETS = (0, -1, 1, -2, 2, -3, 3, -4)


def attention_kernel(
    doc_ref, q_hbm, k_hbm, v_hbm, o_ref,
    even, odd, parcel, q_ref, acc, peak, first,
    load_sem, piece_sem, opposite_sem, relay_sem, start_sem, across_sem, behind_sem, ahead_sem, core_sem,
):
    seq, head = lax.axis_index("seq"), lax.axis_index("head")
    core, y, x = lax.rem(seq, 2), lax.rem(seq // 2, 4), seq // 8
    z, half = lax.rem(head, 8), head // 8
    chip = x * 4 + y
    halves = (half, 1 - half)

    def at(chip_to, core_to, half_to, z_to):
        return (lax.rem(chip_to, 8) * 2 + core_to, half_to * 8 + lax.rem(z_to, 8))

    def along(off):
        return at(chip, core, half, z + (off + 8))

    swap_to = at(chip, core, 1 - half, z)
    across_to = at(chip + 4, core, half, z)
    opposite_to = at(chip + 2, core, half, z)
    opposite_from = at(chip + 6, core, half, z)
    up_to = at(x * 4 + lax.rem(y + 1, 4), core, half, z)
    down_to = at(x * 4 + lax.rem(y + 3, 4), core, half, z)
    core_to = at(chip, 1 - core, half, z)

    barrier = pltpu.get_barrier_semaphore()
    partners = (along(-1), along(1), along(-2), along(2), swap_to, across_to, up_to, down_to, opposite_from, core_to)
    for partner in partners:
        pl.semaphore_signal(barrier, inc=1, device_id=partner, device_id_type=MESH)

    mine = pl.ds(pl.multiple_of(half * PIECE, PIECE), PIECE)
    theirs = pl.ds(pl.multiple_of((1 - half) * PIECE, PIECE), PIECE)
    rows_of = (mine, theirs)
    loads = []
    for side in range(2):
        for n, ref in enumerate((k_hbm, v_hbm)):
            loads.append(pltpu.make_async_copy(ref.at[halves[side]], parcel.at[side, n], load_sem.at[side * 2 + n]))
    own_loads = [
        pltpu.make_async_copy(ref.at[half], even.at[z, OWN, n, mine, :], load_sem.at[4 + n])
        for n, ref in enumerate((k_hbm, v_hbm))
    ]
    q_load = pltpu.make_async_copy(q_hbm.at[0], q_ref, load_sem.at[6])
    for one in loads + own_loads + [q_load]:
        one.start()

    start = seq * SHARD
    lane = lax.broadcasted_iota(jnp.int32, (1, 128), 1)
    place = jnp.where(lane < PIECE, lane, lane + (SHARD // 2 - PIECE))
    peak[...] = jnp.full_like(peak, HIDDEN)
    acc[...] = jnp.zeros_like(acc)
    pos = start + lax.broadcasted_iota(jnp.int32, (SHARD, 128), 0)
    doc_first = jnp.zeros((SHARD, 128), jnp.int32)
    begin = jnp.int32(0)
    for d in range(doc_ref.shape[0]):
        doc_first = jnp.where(pos >= begin, begin, doc_first)
        begin = begin + doc_ref[d]
    first[...] = doc_first - place

    for one in loads:
        one.wait()
    pl.semaphore_wait(barrier, len(partners))

    slice_of = [lax.rem(z + off + 8, 8) for off in OFFSETS]
    started = []

    def copy(src, dst, sems, index, to):
        return pltpu.make_async_remote_copy(
            src_ref=src, dst_ref=dst, send_sem=sems.at[(0,) + index], recv_sem=sems.at[(1,) + index],
            device_id=to, device_id_type=MESH,
        )

    def send(copies):
        for one in copies:
            one.start()
            started.append(one)

    def swap(rows):
        return copy(parcel.at[1], even.at[z, OWN, :, rows, :], piece_sem, (1, 0), swap_to)

    def side_ref(u, side, slot=OWN):
        return even.at[slice_of[u], slot, :, rows_of[side], :]

    def side_source(side):
        return parcel.at[0] if side == 0 else side_ref(0, 1)

    def pieces_out(side):
        out = [
            copy(side_source(side), side_ref(0, side, slot), start_sem, (side, slot), to)
            for slot, to in ((ACROSS, across_to), (OPPOSITE, opposite_to))
        ]
        for u in (1, 2, 3, 4):
            out.append(copy(side_source(side), side_ref(0, side), piece_sem, (side, u), along(-OFFSETS[u])))
        return out

    def piece_in(u, side):
        return copy(side_source(side), side_ref(u, side), piece_sem, (side, u), along(OFFSETS[u]))

    def start_in(slot, side):
        return copy(side_source(side), side_ref(0, side, slot), start_sem, (side, slot), across_to)

    def spread(u, unit):
        ref = even.at[slice_of[unit], OPPOSITE]
        return copy(ref, ref, opposite_sem, (u - 1,), along(-OFFSETS[u]))

    def relay(slot, n, unit, off):
        ref = even.at[slice_of[unit], slot]
        if n >= 2:
            ref = ref.at[n - 2]
        return copy(ref, ref, relay_sem, (slot, n), along(off))

    def relays_out(slot, unit):
        if OFFSETS[unit] == -2:
            return [relay(slot, 0, unit, 1), relay(slot, 2, unit, 2)]
        if OFFSETS[unit] == 2:
            return [relay(slot, 1, unit, -1), relay(slot, 3, unit, -2)]
        return []

    def relays_in(slot, u):
        for n in {5: (0,), 6: (1,), 7: (2, 3)}[u]:
            relay(slot, n, u, 1).wait_recv()

    def across(u):
        return copy(even.at[slice_of[u], OWN], even.at[slice_of[u], ACROSS], across_sem, (u - 1,), across_to)

    up_slot = jnp.where(y == 3, ACROSS, OWN)
    down_slot = jnp.where(y == 0, OWN, ACROSS)

    def up(u):
        return copy(even.at[slice_of[u], up_slot], even.at[slice_of[u], BEHIND], behind_sem, (u,), up_to)

    def down(u):
        return copy(even.at[slice_of[u], down_slot], even.at[slice_of[u], AHEAD], ahead_sem, (u,), down_to)

    def to_core(u):
        return copy(even.at[slice_of[u], pl.ds(core, 4)], odd.at[slice_of[u]], core_sem, (u,), core_to)

    def own_arrives(*units):
        for u in units:
            if u == 0:
                swap(theirs).wait_recv()
                send(pieces_out(1))
            elif u < 5:
                for side in range(2):
                    piece_in(u, side).wait_recv()
                send(relays_out(OWN, u))
            else:
                relays_in(OWN, u)
            if u:
                send([across(u)])

    def across_arrives(*units):
        for u in units:
            if u:
                across(u).wait_recv()
            else:
                for side in range(2):
                    start_in(ACROSS, side).wait_recv()
            send([up(u), down(u)])

    def opposite_arrives(*units):
        for u in units:
            if u == 0:
                for side in range(2):
                    start_in(OPPOSITE, side).wait_recv()
                send([spread(n, 0) for n in (1, 2, 3, 4)])
            elif u < 5:
                spread(u, u).wait_recv()
                send(relays_out(OPPOSITE, u))
            else:
                relays_in(OPPOSITE, u)

    def sides_arrive(*units):
        for u in units:
            up(u).wait_recv()
            down(u).wait_recv()
            send([to_core(u)])

    def core_arrives(*units):
        for u in units:
            to_core(u).wait_recv()

    send([swap(mine)])
    send(pieces_out(0))
    for one in own_loads + [q_load]:
        one.wait()

    def base(slot, u, from_sibling):
        if from_sibling:
            back = jnp.where(core == 1, BACK[slot], BACK[slot + 1])
            owner = chip - back
            shard = owner * 2 + (1 - core)
        else:
            owner = chip - BACK[slot]
            shard = owner * 2 + core
        return jnp.where(owner >= 0, shard * SHARD + slice_of[u] * PIECE, FAR)

    def attend(keys, values, bases, causal, blocks, block=BLOCK):
        groups = len(bases)
        values = jnp.concatenate([values, jnp.ones_like(values)], axis=1)

        def score(i):
            return lax.dot_general(q_ref[pl.ds(i * block, block), :], keys, NT, preferred_element_type=jnp.float32)

        ahead = score(blocks[0])
        for n, i in enumerate(blocks):
            s = ahead
            ahead = score(blocks[n + 1]) if n + 1 < len(blocks) else None
            r = pl.ds(i * block, block)
            f = first[r, :]
            if causal:
                line = start + i * block + lax.broadcasted_iota(jnp.int32, (block, 128), 0) - place
            cols = []
            for g in range(groups):
                seen = f <= bases[g]
                if causal:
                    seen = seen & (line >= bases[g])
                cols.append(jnp.where(seen, s[:, g * UNIT:(g + 1) * UNIT], HIDDEN))
            top = tree(jnp.maximum, cols)
            old = peak[r, :]
            new = jnp.maximum(old, jnp.max(top, axis=1, keepdims=True))
            shift = new * LOG_SCALE
            factor = jnp.exp2(old * LOG_SCALE - shift)
            peak[r, :] = new
            weights = [jnp.exp2(c * LOG_SCALE - shift) for c in cols]
            p = jnp.concatenate([w.astype(jnp.bfloat16) for w in weights], axis=1)
            product = lax.dot_general(p, values, NN, preferred_element_type=jnp.float32)
            for part in (pl.ds(0, 128), pl.ds(128, 128)):
                acc[r, part] = acc[r, part] * factor + product[:, part.start:part.start + 128]

    def attend_own(units):
        keys, values = [[even[slice_of[u], OWN, n, pl.ds(0, PIECE)] for u in units] for n in range(2)]
        bases = [
            jnp.where(lane < PIECE, base(OWN, a, False), base(OWN, b, False) - SHARD // 2)
            for a, b in zip(units[::2], units[1::2])
        ]
        attend(jnp.concatenate(keys, axis=0), jnp.concatenate(values, axis=0), bases, True, (0, 1))
        keys, values = [[even[slice_of[u], OWN, n] for u in units] for n in range(2)]
        bases = [base(OWN, u, False) for u in units]
        attend(jnp.concatenate(keys, axis=0), jnp.concatenate(values, axis=0), bases, True, (2, 3))

    def attend_others(seen_even, seen_odd, blocks=(0, 1, 2, 3), block=BLOCK):
        keys, values, bases = [], [], []
        for ref, slots, units in ((even, range(1, 5), seen_even), (odd, range(4), seen_odd)):
            for u in units:
                for slot in slots:
                    keys.append(ref[slice_of[u], slot, 0])
                    values.append(ref[slice_of[u], slot, 1])
                    bases.append(base(slot, u, ref is odd))
        attend(jnp.concatenate(keys, axis=0), jnp.concatenate(values, axis=0), bases, False, blocks, block)

    own_arrives(0)
    own_arrives(1)
    own_arrives(2)
    own_arrives(3)
    own_arrives(4)
    across_arrives(0)
    opposite_arrives(0)
    attend_own((0, 1, 2, 3))
    across_arrives(1)
    across_arrives(2)
    own_arrives(5)
    own_arrives(6)
    own_arrives(7)
    sides_arrive(0)
    attend_others((0,), ())
    across_arrives(3)
    across_arrives(4)
    opposite_arrives(1, 2)
    opposite_arrives(3, 4)
    attend_own((4, 5, 6, 7))
    sides_arrive(1)
    sides_arrive(2)
    core_arrives(0)
    across_arrives(5)
    across_arrives(6)
    attend_others((1, 2), (0,), (0, 1))
    across_arrives(7)
    attend_others((1, 2), (0,), (2, 3))
    sides_arrive(3)
    sides_arrive(4)
    opposite_arrives(5, 6, 7)
    core_arrives(1, 2)
    attend_others((3, 4), (1, 2), (0, 1))
    sides_arrive(5)
    sides_arrive(6)
    sides_arrive(7)
    attend_others((3, 4), (1, 2), (2, 3))
    core_arrives(3, 4)
    attend_others((5, 6, 7), (3, 4), (0, 1), 2 * BLOCK)
    core_arrives(5, 6, 7)
    attend_others((), (5, 6, 7), (0, 1), 2 * BLOCK)
    o_ref[0] = (acc[:, :128] / acc[:, 128:]).astype(o_ref.dtype)
    for one in started:
        one.wait_send()


def tree(join, parts):
    while len(parts) > 1:
        rest = [parts[-1]] if len(parts) % 2 else []
        parts = [join(a, b) for a, b in zip(parts[::2], parts[1::2])] + rest
    return parts[0]


def local(query_heads, key_heads, value_heads, doc_lengths):
    _, rows, width = query_heads.shape
    vmem = pl.BlockSpec(memory_space=pltpu.VMEM)

    hbm = pl.BlockSpec(memory_space=pltpu.HBM)

    def sems(*n):
        return pltpu.SemaphoreType.DMA((2,) + n)

    return pl.pallas_call(
        attention_kernel,
        out_shape=jax.ShapeDtypeStruct(query_heads.shape, jnp.bfloat16),
        in_specs=[pl.BlockSpec(memory_space=pltpu.SMEM), hbm, hbm, hbm],
        out_specs=vmem,
        scratch_shapes=[
            pltpu.VMEM((8, 5, 2, UNIT, width), jnp.bfloat16),
            pltpu.VMEM((8, 4, 2, UNIT, width), jnp.bfloat16),
            pltpu.VMEM((2, 2, PIECE, width), jnp.bfloat16),
            pltpu.VMEM((rows, width), jnp.bfloat16),
            pltpu.VMEM((rows, 2 * width), jnp.float32),
            pltpu.VMEM((rows, 128), jnp.float32),
            pltpu.VMEM((rows, 128), jnp.int32),
            pltpu.SemaphoreType.DMA((7,)),
            sems(2, 5), sems(4), sems(2, 4), sems(2, 5), sems(7), sems(8), sems(8), sems(8),
        ],
        compiler_params=pltpu.CompilerParams(
            collective_id=0, has_side_effects=True, vmem_limit_bytes=65000 * 2**10
        ),
        name="attention",
    )(doc_lengths, query_heads, key_heads, value_heads)


def solution(mesh):
    placed = (
        P("head", "seq", None),
        P(None, ("seq", "head"), None),
        P(None, ("seq", "head"), None),
        P(),
    )
    return jax.shard_map(
        local, mesh=mesh, in_specs=placed, out_specs=P("head", "seq", None), check_vma=False
    )
```
